512 devices in a mesh: dp: 32 (over x, y), tensor: 16 (over z, core).
Axes of the slice: x: 4, y: 8, z: 8, core: 2. Of those that a mesh axis runs over, the one named last changes fastest.
Arguments:
- gate_pre: bfloat16 [2, 4096, 53248], P(None, 'dp', 'tensor'), parts along dimension 1, may hold values from -8 to 8
- up_pre: bfloat16 [2, 4096, 53248], P(None, 'dp', 'tensor'), parts along dimension 1, may hold values from -8 to 8
- rotation52: bfloat16 [52, 52], replicated, may hold values from -0.875 to 0.875
Outputs:
- quantized: bfloat16 [2, 4096, 53248], P(None, 'dp', 'tensor'), parts along dimension 1
- peaks: float32 [2, 4096], P(None, 'dp'), parts along dimension 1
The draws below stay inside these ranges and needn't reach their ends.
There are 32 independent parts, one for each index of `dp`. The reference program is written for one: setup_inputs(seed, part) draws one part's arguments, and reference() takes and returns one part's arrays. A program takes and returns all parts, laid end to end along the dimension named above; an argument that names none is the same for every part. Nothing has to cross between parts.
All inputs are finite; a program needn't handle non-finite values. Where the reference program divides by a largest or mean magnitude, that divisor is 1e-20 or more.
Results may differ from the reference program's by a relative error of at most 0.005.
Values may be sent and summed in bfloat16 or wider, within the bound.
No kernel may reach another device: no remote copies, remote signals or barrier semaphores. Data moves between devices by JAX's collectives and lax.ppermute only.
A program may use at most 128 MiB of HBM per device.

```python
import jax
import jax.numpy as jnp
from jax import lax

FF = 53248
HAD_SMALL = 52
HAD_BIG = 1024
ROWS = 128
STEPS = 2


def block_levels(own_key, shape, cuts, least, largest):
    factor_of, own = 1.0, jax.random.fold_in(own_key, 6)
    for axis_at, parts in cuts:
        draws = jnp.exp(jax.random.uniform(jax.random.fold_in(own, axis_at), (parts,), jnp.float32, least / len(cuts), largest / len(cuts)))
        factor_of = factor_of * jnp.repeat(draws, shape[axis_at] // parts).reshape([-1 if axis == axis_at else 1 for axis in range(len(shape))])
    return factor_of


def normal_values(key, extent, width, most, pieces=(), kind=jnp.bfloat16):
    result = jax.random.normal(key, extent, jnp.float32) * width
    if len(pieces) > 0:
        result = block_levels(key, extent, pieces, -0.22, 0.18) * result
    return jnp.clip(result, min=-most, max=most).astype(kind)


def setup_inputs(seed: int = 0, part: int = 0) -> dict:
    splits = jax.random.split(jax.random.key(seed), 4)
    own_keys = jax.random.split(jax.random.fold_in(splits[3], part), 4)
    return {
        "gate_pre": normal_values(own_keys[0], (STEPS, ROWS, FF), 1.5, 8.0, ((2, 16),)),
        "up_pre": normal_values(own_keys[1], (STEPS, ROWS, FF), 1.0, 8.0, ((2, 16),)),
        "rotation52": normal_values(splits[2], (HAD_SMALL, HAD_SMALL), HAD_SMALL ** -0.5, 0.875),
    }


def sylvester(order):
    index = jnp.arange(order, dtype=jnp.int32)
    parity = jnp.zeros((order, order), jnp.int32)
    for level in range(order.bit_length() - 1):
        parity = parity + jnp.right_shift(index[:, None], level) % 2 * (jnp.right_shift(index[None, :], level) % 2)
    return (1 - 2 * (parity % 2)).astype(jnp.float32)


def kron_hadamard(mixed, order):
    bits = order.bit_length() - 1
    high = 2 ** (bits // 2)
    low = order // high
    steps, rows, _, cols = mixed.shape
    split = mixed.reshape(steps, rows, high, low, cols)
    split = jnp.einsum("srhlc,hk->srklc", split, sylvester(high), precision=lax.Precision.HIGHEST)
    split = jnp.einsum("srklc,lm->srkmc", split, sylvester(low), precision=lax.Precision.HIGHEST)
    return split.reshape(steps, rows, order, cols)


def reference(gate_pre, up_pre, rotation52):
    hidden = (jax.nn.silu(gate_pre.astype(jnp.float32)) * up_pre.astype(jnp.float32)).astype(jnp.bfloat16)
    blocks = hidden.reshape(STEPS, ROWS, HAD_BIG, HAD_SMALL).astype(jnp.float32)
    mixed = jnp.einsum("srba,ac->srbc", blocks, rotation52.astype(jnp.float32), precision=lax.Precision.HIGHEST)
    rotated = kron_hadamard(mixed, HAD_BIG) * (HAD_BIG ** -0.5)
    peaks = jnp.max(jnp.abs(rotated), axis=(2, 3)) + 1e-6
    quantized = (rotated / peaks[:, :, None, None]).astype(jnp.bfloat16).reshape(STEPS, ROWS, FF)
    return quantized, peaks
```

```python
import jax
import jax.numpy as jnp
from jax import lax
from jax.experimental import pallas as pl
from jax.experimental.pallas import tpu as pltpu
from jax.sharding import PartitionSpec as P

HAD_BIG = 1024
LOW = 32
LANES = 128
VMEM_LIMIT = 48 * 1024 * 1024


def parity_sign(left, right):
    both = left & right
    parity = both
    for level in (1, 2, 3, 4):
        parity = parity ^ (both >> level)
    return 1 - 2 * (parity & 1)


def factor_kernel(rotation_ref, out_ref):
    small = rotation_ref.shape[0]
    width = out_ref.shape[0]
    f32, bf16 = jnp.float32, jnp.bfloat16

    def expand(rows, shape, offset, dim):
        index = lax.broadcasted_iota(jnp.int32, shape, dim) + offset
        other = lax.broadcasted_iota(jnp.int32, shape, 1 - dim)
        block = (index * 1261) >> 16
        value = block if rows else index - block * small
        return (value == other).astype(f32).astype(bf16)

    tiled = jnp.dot(
        rotation_ref[...], expand(False, (small, width), 0, 1), preferred_element_type=f32
    ).astype(bf16)
    big = lax.broadcasted_iota(jnp.int32, (LOW, width), 0)
    lane = lax.broadcasted_iota(jnp.int32, (LOW, width), 1)
    signs = parity_sign(big, (lane * 1261) >> 16).astype(f32).astype(bf16)

    @pl.loop(0, width // LANES)
    def _(step):
        start = pl.multiple_of(step * LANES, LANES)
        value = jnp.dot(expand(False, (LANES, small), start, 0), tiled, preferred_element_type=f32)
        sign = jnp.dot(expand(True, (LANES, LOW), start, 0), signs, preferred_element_type=f32)
        out_ref[pl.ds(start, LANES), :] = (value * sign).astype(bf16)


def factor(rotation52):
    width = LOW * rotation52.shape[0]
    return pl.pallas_call(
        factor_kernel,
        out_shape=jax.ShapeDtypeStruct((width, width), jnp.bfloat16),
        in_specs=[pl.BlockSpec(memory_space=pltpu.VMEM)],
        out_specs=pl.BlockSpec(memory_space=pltpu.VMEM),
        compiler_params=pltpu.CompilerParams(vmem_limit_bytes=VMEM_LIMIT),
        cost_estimate=pl.CostEstimate(
            flops=2 * width * width * 84, bytes_accessed=2 * width * width, transcendentals=0
        ),
        name="kron_factor",
    )(rotation52)


def butterfly(values):
    count = len(values)
    distance = 1
    while distance < count:
        values = [
            values[i] + values[i ^ distance] if i & distance == 0 else values[i ^ distance] - values[i]
            for i in range(count)
        ]
        distance *= 2
    return values


def transform_kernel(hidden_ref, factor_ref, out_ref, product_ref, rotated_ref):
    groups, rows, width = hidden_ref.shape
    low = factor_ref.shape[0]
    halves = width // low
    f32 = jnp.float32
    peak = [jnp.zeros((8, LANES), f32) for _ in range(rows // 8)]
    for start in range(0, low, 2 * LANES):
        span = min(2 * LANES, low - start)
        for half in range(halves):
            product_ref[half, :, :, :span] = jnp.dot(
                hidden_ref[:, :, half * low : (half + 1) * low].reshape(groups * rows, low),
                factor_ref[:, start : start + span],
                preferred_element_type=f32,
            ).reshape(groups, rows, span)
        for part in range(rows // 8):
            at = slice(part * 8, part * 8 + 8)
            for lane in range(0, span, LANES):
                values = butterfly(
                    [
                        product_ref[half, group, at, lane : lane + LANES]
                        for group in range(groups)
                        for half in range(halves)
                    ]
                )
                for i, value in enumerate(values):
                    group, half = divmod(i, halves)
                    column = half * low + start + lane
                    rotated_ref[group, at, column : column + LANES] = value
                    peak[part] = jnp.maximum(peak[part], jnp.abs(value))
    scale = HAD_BIG**-0.5
    largest = jnp.concatenate([jnp.max(p, axis=1, keepdims=True) for p in peak], axis=0)
    largest = largest * scale + 1e-6
    inverse = scale / largest
    coarse = largest.astype(jnp.bfloat16).astype(f32)
    lanes = lax.broadcasted_iota(jnp.int32, (rows, LANES), 1)
    parts = jnp.where(lanes == 0, coarse, largest - coarse).astype(jnp.bfloat16)
    for group in range(groups):
        out_ref[group, :, :width] = (rotated_ref[group] * inverse).astype(out_ref.dtype)
        out_ref[group, :, width:] = parts


def transform(hidden, weights):
    groups, rows, width = hidden.shape
    low = weights.shape[0]
    return pl.pallas_call(
        transform_kernel,
        out_shape=jax.ShapeDtypeStruct((groups, rows, width + LANES), jnp.bfloat16),
        in_specs=[pl.BlockSpec(memory_space=pltpu.VMEM)] * 2,
        out_specs=pl.BlockSpec(memory_space=pltpu.VMEM),
        scratch_shapes=[
            pltpu.VMEM((width // low, groups, rows, 2 * LANES), jnp.float32),
            pltpu.VMEM((groups, rows, width), jnp.float32),
        ],
        compiler_params=pltpu.CompilerParams(vmem_limit_bytes=VMEM_LIMIT),
        cost_estimate=pl.CostEstimate(
            flops=2 * groups * rows * width * low,
            bytes_accessed=4 * groups * rows * width + 2 * low * low,
            transcendentals=0,
        ),
        name="rotate_rows",
    )(hidden, weights)


def body(gate_pre, up_pre, rotation52):
    steps, rows, width = gate_pre.shape
    groups = lax.axis_size("tensor")
    f32 = jnp.float32
    weights = factor(rotation52)
    hidden = (jax.nn.silu(gate_pre.astype(f32)) * up_pre.astype(f32)).astype(jnp.bfloat16)
    hidden = hidden.reshape(groups, steps * rows // groups, width)
    mine = lax.all_to_all(hidden, "tensor", 0, 0)
    packed = lax.all_to_all(transform(mine, weights), "tensor", 0, 0)
    quantized = packed[:, :, :width].reshape(steps, rows, width)
    peaks = packed[:, :, width].astype(f32) + packed[:, :, width + 1].astype(f32)
    return (quantized, peaks.reshape(steps, rows))


def solution(mesh):
    in_specs = (P(None, "dp", "tensor"), P(None, "dp", "tensor"), P())
    out_specs = (P(None, "dp", "tensor"), P(None, "dp"))
    return jax.shard_map(body, mesh=mesh, in_specs=in_specs, out_specs=out_specs, check_vma=False)
```

```python
import jax
import jax.numpy as jnp
from jax import lax
from jax.experimental import pallas as pl
from jax.experimental.pallas import tpu as pltpu
from jax.sharding import PartitionSpec as P

HAD_BIG = 1024
LOW = 32
LANES = 128
TILE = 2 * LANES
VMEM_LIMIT = 20 * 1024 * 1024
STREAM_LIMIT = 58 * 1024 * 1024


def hidden_kernel(gate_hbm, up_hbm, out_ref, gate_ref, up_ref, sems):
    chunks, rows, width = gate_ref.shape
    f32 = jnp.float32
    copies = []
    for chunk in range(chunks):
        at = pl.ds(chunk * rows, rows)
        for k, (source, target) in enumerate(((gate_hbm, gate_ref), (up_hbm, up_ref))):
            copy = pltpu.make_async_copy(source.at[at], target.at[chunk], sems.at[chunk, k])
            copy.start()
            copies.append(copy)
    for chunk in range(chunks):
        copies[2 * chunk].wait()
        copies[2 * chunk + 1].wait()

        @pl.loop(0, rows // 16)
        def _(step):
            at = pl.ds(pl.multiple_of(step * 16, 16), 16)
            gate = gate_ref[chunk, at].astype(f32)
            half = 0.5 * gate
            silu = half * jnp.tanh(half) + half
            value = (silu * up_ref[chunk, at].astype(f32)).astype(out_ref.dtype)
            out_ref[pl.ds(pl.multiple_of(chunk * rows + step * 16, 16), 16), :] = value


def gated(gate, up):
    rows, width = gate.shape
    chunks = 4
    held = pltpu.VMEM((chunks, rows // chunks, width), gate.dtype)
    return pl.pallas_call(
        hidden_kernel,
        out_shape=jax.ShapeDtypeStruct(gate.shape, gate.dtype),
        in_specs=[pl.BlockSpec(memory_space=pl.ANY)] * 2,
        out_specs=pl.BlockSpec(memory_space=pltpu.VMEM),
        scratch_shapes=[held, held, pltpu.SemaphoreType.DMA((chunks, 2))],
        compiler_params=pltpu.CompilerParams(vmem_limit_bytes=STREAM_LIMIT),
        cost_estimate=pl.CostEstimate(
            flops=6 * rows * width, bytes_accessed=6 * rows * width, transcendentals=rows * width
        ),
        name="gated_hidden",
    )(gate, up)


def unpack_kernel(packed_ref, out_hbm, peak_ref, sem):
    groups, rows, packed = packed_ref.shape
    width = out_hbm.shape[2]
    steps, span = peak_ref.shape
    per = groups // steps
    copies = []
    count = sem.shape[0]
    for part in range(count):
        at = pl.ds(part * (groups // count), groups // count)
        copy = pltpu.make_async_copy(
            packed_ref.at[at, :, pl.ds(0, width)], out_hbm.at[at], sem.at[part]
        )
        copy.start()
        copies.append(copy)
    lanes = lax.broadcasted_iota(jnp.int32, (8, packed - width), 1)
    both = (lanes < 2).astype(jnp.float32).astype(jnp.bfloat16)
    for step in range(steps):
        parts = packed_ref[step * per : step * per + per, :, width:].reshape(span, packed - width)
        sums = lax.dot_general(
            both, parts, (((1,), (1,)), ((), ())), preferred_element_type=jnp.float32
        )
        peak_ref[step : step + 1, :] = sums[:1]
    for copy in copies:
        copy.wait()


def unpack(packed, steps, span, width):
    quantized, peaks = pl.pallas_call(
        unpack_kernel,
        out_shape=(
            jax.ShapeDtypeStruct((*packed.shape[:2], width), packed.dtype),
            jax.ShapeDtypeStruct((steps, span), jnp.float32),
        ),
        in_specs=[pl.BlockSpec(memory_space=pltpu.VMEM)],
        out_specs=(pl.BlockSpec(memory_space=pl.ANY), pl.BlockSpec(memory_space=pltpu.VMEM)),
        scratch_shapes=[pltpu.SemaphoreType.DMA((4,))],
        compiler_params=pltpu.CompilerParams(vmem_limit_bytes=VMEM_LIMIT),
        name="unpack",
    )(packed)
    return quantized.reshape(steps, span, width), peaks


def parity_sign(left, right):
    both = left & right
    parity = both
    for level in (1, 2, 3, 4):
        parity = parity ^ (both >> level)
    return 1 - 2 * (parity & 1)


def factor_kernel(rotation_ref, base_ref, sign_ref):
    small = rotation_ref.shape[0]
    height, width = base_ref.shape
    f32, bf16 = jnp.float32, jnp.bfloat16

    def block(index):
        return (index * 1261) >> 16

    def iota(shape, dim):
        return lax.broadcasted_iota(jnp.int32, shape, dim)

    def one_where(mask):
        return mask.astype(f32).astype(bf16)

    lane = iota((small, width), 1)
    across = one_where(lane - block(lane) * small == iota((small, width), 0))
    tiled = jnp.dot(rotation_ref[...], across, preferred_element_type=f32).astype(bf16)
    row = iota((height, small), 0)
    down = one_where(row - block(row) * small == iota((height, small), 1))
    value = jnp.dot(down, tiled, preferred_element_type=f32)
    shape = (height, width)
    sign = parity_sign(block(iota(shape, 0)), block(iota(shape, 1))).astype(f32)
    base_ref[...] = (value * sign).astype(bf16)
    shape = sign_ref.shape
    sign_ref[...] = parity_sign(4 * iota(shape, 0), block(iota(shape, 1))).astype(f32).astype(bf16)


def factor(rotation52):
    small = rotation52.shape[0]
    width = LOW * small
    return pl.pallas_call(
        factor_kernel,
        out_shape=(
            jax.ShapeDtypeStruct((4 * small, width), jnp.bfloat16),
            jax.ShapeDtypeStruct((16, width), jnp.bfloat16),
        ),
        in_specs=[pl.BlockSpec(memory_space=pltpu.VMEM)],
        out_specs=[pl.BlockSpec(memory_space=pltpu.VMEM)] * 2,
        compiler_params=pltpu.CompilerParams(vmem_limit_bytes=VMEM_LIMIT),
        cost_estimate=pl.CostEstimate(
            flops=2 * 4 * small * width * 52, bytes_accessed=8 * small * width, transcendentals=0
        ),
        name="kron_factor",
    )(rotation52)


def butterfly(values):
    count = len(values)
    distance = 1
    while distance < count:
        values = [
            values[i] + values[i ^ distance] if i & distance == 0 else values[i ^ distance] - values[i]
            for i in range(count)
        ]
        distance *= 2
    return values


def transform_kernel(hidden_ref, base_ref, sign_ref, out_ref, factor_ref, product_ref, rotated_ref):
    groups, rows, width = hidden_ref.shape
    height, low = base_ref.shape
    halves = width // low
    f32 = jnp.float32
    starts = list(range(0, low, TILE))
    peak = [jnp.zeros((8, LANES), f32) for _ in range(rows // 8)]

    def expand(n):
        size = min(TILE, low - starts[n])
        at = slice(starts[n], starts[n] + size)
        for i in range(low // height):
            factor_ref[n % 2, i * height : (i + 1) * height, :size] = (
                base_ref[:, at] * sign_ref[i : i + 1, at]
            )

    def multiply(n):
        size = min(TILE, low - starts[n])
        for half in range(halves):
            product_ref[n % 2, half, :, :, :size] = jnp.dot(
                hidden_ref[:, :, half * low : (half + 1) * low].reshape(groups * rows, low),
                factor_ref[n % 2, :, :size],
                preferred_element_type=f32,
            ).reshape(groups, rows, size)

    def combine(n):
        for part in range(rows // 8):
            at = slice(part * 8, part * 8 + 8)
            for lane in range(0, min(TILE, low - starts[n]), LANES):
                values = butterfly(
                    [
                        product_ref[n % 2, half, group, at, lane : lane + LANES]
                        for group in range(groups)
                        for half in range(halves)
                    ]
                )
                for i, value in enumerate(values):
                    group, half = divmod(i, halves)
                    column = half * low + starts[n] + lane
                    rotated_ref[group, at, column : column + LANES] = value
                sizes = [jnp.abs(value) for value in values] + [peak[part]]
                while len(sizes) > 1:
                    sizes = [jnp.maximum(*sizes[:2])] + sizes[2:]
                peak[part] = sizes[0]

    expand(0)
    for n in range(len(starts)):
        if n + 1 < len(starts):
            expand(n + 1)
        multiply(n)
        if n > 0:
            combine(n - 1)
    combine(len(starts) - 1)
    scale = HAD_BIG**-0.5
    largest = jnp.concatenate([jnp.max(p, axis=1, keepdims=True) for p in peak], axis=0)
    largest = largest * scale + 1e-6
    inverse = scale / largest
    coarse = largest.astype(jnp.bfloat16).astype(f32)
    lanes = lax.broadcasted_iota(jnp.int32, (rows, LANES), 1)
    parts = jnp.where(lanes == 0, coarse, jnp.where(lanes == 1, largest - coarse, 0.0))
    parts = parts.astype(jnp.bfloat16)
    for group in range(groups):
        out_ref[group, :, :width] = (rotated_ref[group] * inverse).astype(out_ref.dtype)
        out_ref[group, :, width:] = parts


def transform(hidden, base, sign):
    groups, rows, width = hidden.shape
    low = base.shape[1]
    return pl.pallas_call(
        transform_kernel,
        out_shape=jax.ShapeDtypeStruct((groups, rows, width + LANES), jnp.bfloat16),
        in_specs=[pl.BlockSpec(memory_space=pltpu.VMEM)] * 3,
        out_specs=pl.BlockSpec(memory_space=pltpu.VMEM),
        scratch_shapes=[
            pltpu.VMEM((2, low, TILE), jnp.bfloat16),
            pltpu.VMEM((2, width // low, groups, rows, TILE), jnp.float32),
            pltpu.VMEM((groups, rows, width), jnp.float32),
        ],
        compiler_params=pltpu.CompilerParams(vmem_limit_bytes=VMEM_LIMIT),
        cost_estimate=pl.CostEstimate(
            flops=2 * groups * rows * width * low,
            bytes_accessed=4 * groups * rows * width,
            transcendentals=0,
        ),
        name="rotate_rows",
    )(hidden, base, sign)


def body(gate_pre, up_pre, rotation52):
    steps, rows, width = gate_pre.shape
    groups = lax.axis_size("tensor")
    base, sign = factor(rotation52)
    flat = (steps * rows, width)
    hidden = gated(gate_pre.reshape(flat), up_pre.reshape(flat))
    mine = lax.all_to_all(hidden.reshape(groups, -1, width), "tensor", 0, 0)
    packed = lax.all_to_all(transform(mine, base, sign), "tensor", 0, 0)
    return unpack(packed, steps, rows, width)


def solution(mesh):
    in_specs = (P(None, "dp", "tensor"), P(None, "dp", "tensor"), P())
    out_specs = (P(None, "dp", "tensor"), P(None, "dp"))
    return jax.shard_map(body, mesh=mesh, in_specs=in_specs, out_specs=out_specs, check_vma=False)
```

```python
import jax
import jax.numpy as jnp
from jax import lax
from jax.experimental import pallas as pl
from jax.experimental.pallas import tpu as pltpu
from jax.sharding import PartitionSpec as P

HAD_BIG = 1024
LOW = 32
LANES = 128
TILE = 2 * LANES
VMEM_LIMIT = 20 * 1024 * 1024
STREAM_LIMIT = 58 * 1024 * 1024


def hidden_kernel(gate_hbm, up_hbm, out_hbm, gate_ref, up_ref, out_ref, sems):
    chunks, rows, width = gate_ref.shape
    f32 = jnp.float32
    block = 32
    copies = []
    for chunk in range(chunks):
        at = pl.ds(chunk * rows, rows)
        for k, (source, target) in enumerate(((gate_hbm, gate_ref), (up_hbm, up_ref))):
            copy = pltpu.make_async_copy(source.at[at], target.at[chunk], sems.at[chunk, k])
            copy.start()
            copies.append(copy)
    results = []
    for chunk in range(chunks):
        copies[2 * chunk].wait()
        copies[2 * chunk + 1].wait()

        @pl.loop(0, rows // block)
        def _(step):
            at = pl.ds(pl.multiple_of(step * block, block), block)
            gate = gate_ref[chunk, at].astype(f32)
            half = 0.5 * gate
            silu = half * jnp.tanh(half) + half
            out_ref[chunk, at] = (silu * up_ref[chunk, at].astype(f32)).astype(out_ref.dtype)

        at = pl.ds(chunk * rows, rows)
        result = pltpu.make_async_copy(out_ref.at[chunk], out_hbm.at[at], sems.at[chunk, 2])
        result.start()
        results.append(result)
    for result in results:
        result.wait()


def gated(gate, up):
    rows, width = gate.shape
    chunks = 4
    held = pltpu.VMEM((chunks, rows // chunks, width), gate.dtype)
    return pl.pallas_call(
        hidden_kernel,
        out_shape=jax.ShapeDtypeStruct(gate.shape, gate.dtype),
        in_specs=[pl.BlockSpec(memory_space=pl.ANY)] * 2,
        out_specs=pl.BlockSpec(memory_space=pl.ANY),
        scratch_shapes=[held, held, held, pltpu.SemaphoreType.DMA((chunks, 3))],
        compiler_params=pltpu.CompilerParams(vmem_limit_bytes=STREAM_LIMIT),
        cost_estimate=pl.CostEstimate(
            flops=6 * rows * width, bytes_accessed=6 * rows * width, transcendentals=rows * width
        ),
        name="gated_hidden",
    )(gate, up)


def unpack_kernel(packed_ref, out_hbm, peak_ref, sem):
    groups, rows, packed = packed_ref.shape
    width = out_hbm.shape[2]
    steps, span = peak_ref.shape
    per = groups // steps
    copies = []
    count = sem.shape[0]
    for part in range(count):
        at = pl.ds(part * (groups // count), groups // count)
        copy = pltpu.make_async_copy(
            packed_ref.at[at, :, pl.ds(0, width)], out_hbm.at[at], sem.at[part]
        )
        copy.start()
        copies.append(copy)
    lanes = lax.broadcasted_iota(jnp.int32, (8, packed - width), 1)
    both = (lanes < 2).astype(jnp.float32).astype(jnp.bfloat16)
    for step in range(steps):
        parts = packed_ref[step * per : step * per + per, :, width:].reshape(span, packed - width)
        sums = lax.dot_general(
            both, parts, (((1,), (1,)), ((), ())), preferred_element_type=jnp.float32
        )
        peak_ref[step : step + 1, :] = sums[:1]
    for copy in copies:
        copy.wait()


def unpack(packed, steps, span, width):
    quantized, peaks = pl.pallas_call(
        unpack_kernel,
        out_shape=(
            jax.ShapeDtypeStruct((*packed.shape[:2], width), packed.dtype),
            jax.ShapeDtypeStruct((steps, span), jnp.float32),
        ),
        in_specs=[pl.BlockSpec(memory_space=pltpu.VMEM)],
        out_specs=(pl.BlockSpec(memory_space=pl.ANY), pl.BlockSpec(memory_space=pltpu.VMEM)),
        scratch_shapes=[pltpu.SemaphoreType.DMA((4,))],
        compiler_params=pltpu.CompilerParams(vmem_limit_bytes=VMEM_LIMIT),
        name="unpack",
    )(packed)
    return quantized.reshape(steps, span, width), peaks


def parity_sign(left, right):
    both = left & right
    parity = both
    for level in (1, 2, 3, 4):
        parity = parity ^ (both >> level)
    return 1 - 2 * (parity & 1)


def factor_kernel(rotation_ref, base_ref, sign_ref):
    small = rotation_ref.shape[0]
    height, width = base_ref.shape
    f32, bf16 = jnp.float32, jnp.bfloat16

    def block(index):
        return (index * 1261) >> 16

    def iota(shape, dim):
        return lax.broadcasted_iota(jnp.int32, shape, dim)

    def one_where(mask):
        return mask.astype(f32).astype(bf16)

    lane = iota((small, width), 1)
    across = one_where(lane - block(lane) * small == iota((small, width), 0))
    tiled = jnp.dot(rotation_ref[...], across, preferred_element_type=f32).astype(bf16)
    row = iota((height, small), 0)
    down = one_where(row - block(row) * small == iota((height, small), 1))
    value = jnp.dot(down, tiled, preferred_element_type=f32)
    shape = (height, width)
    sign = parity_sign(block(iota(shape, 0)), block(iota(shape, 1))).astype(f32)
    base_ref[...] = (value * sign).astype(bf16)
    shape = sign_ref.shape
    sign_ref[...] = parity_sign(4 * iota(shape, 0), block(iota(shape, 1))).astype(f32).astype(bf16)


def factor(rotation52):
    small = rotation52.shape[0]
    width = LOW * small
    return pl.pallas_call(
        factor_kernel,
        out_shape=(
            jax.ShapeDtypeStruct((4 * small, width), jnp.bfloat16),
            jax.ShapeDtypeStruct((16, width), jnp.bfloat16),
        ),
        in_specs=[pl.BlockSpec(memory_space=pltpu.VMEM)],
        out_specs=[pl.BlockSpec(memory_space=pltpu.VMEM)] * 2,
        compiler_params=pltpu.CompilerParams(vmem_limit_bytes=VMEM_LIMIT),
        cost_estimate=pl.CostEstimate(
            flops=2 * 4 * small * width * 52, bytes_accessed=8 * small * width, transcendentals=0
        ),
        name="kron_factor",
    )(rotation52)


def butterfly(values):
    count = len(values)
    distance = 1
    while distance < count:
        values = [
            values[i] + values[i ^ distance] if i & distance == 0 else values[i ^ distance] - values[i]
            for i in range(count)
        ]
        distance *= 2
    return values


def transform_kernel(hidden_ref, base_ref, sign_ref, out_ref, factor_ref, product_ref, rotated_ref):
    groups, rows, width = hidden_ref.shape
    height, low = base_ref.shape
    halves = width // low
    f32 = jnp.float32
    starts = list(range(0, low, TILE))
    peak = [jnp.zeros((8, LANES), f32) for _ in range(rows // 8)]

    def expand(n):
        size = min(TILE, low - starts[n])
        at = slice(starts[n], starts[n] + size)
        for i in range(low // height):
            factor_ref[n % 2, i * height : (i + 1) * height, :size] = (
                base_ref[:, at] * sign_ref[i : i + 1, at]
            )

    def multiply(n):
        size = min(TILE, low - starts[n])
        for half in range(halves):
            product_ref[n % 2, half, :, :, :size] = jnp.dot(
                hidden_ref[:, :, half * low : (half + 1) * low].reshape(groups * rows, low),
                factor_ref[n % 2, :, :size],
                preferred_element_type=f32,
            ).reshape(groups, rows, size)

    def combine(n):
        for part in range(rows // 8):
            at = slice(part * 8, part * 8 + 8)
            for lane in range(0, min(TILE, low - starts[n]), LANES):
                values = butterfly(
                    [
                        product_ref[n % 2, half, group, at, lane : lane + LANES]
                        for group in range(groups)
                        for half in range(halves)
                    ]
                )
                for i, value in enumerate(values):
                    group, half = divmod(i, halves)
                    column = half * low + starts[n] + lane
                    rotated_ref[group, at, column : column + LANES] = value
                sizes = [jnp.abs(value) for value in values]
                while len(sizes) > 1:
                    sizes = [jnp.maximum(*pair) for pair in zip(sizes[::2], sizes[1::2])]
                peak[part] = jnp.maximum(peak[part], sizes[0])

    expand(0)
    for n in range(len(starts)):
        if n + 1 < len(starts):
            expand(n + 1)
        multiply(n)
        if n > 0:
            combine(n - 1)
    combine(len(starts) - 1)
    scale = HAD_BIG**-0.5
    largest = jnp.concatenate([jnp.max(p, axis=1, keepdims=True) for p in peak], axis=0)
    largest = largest * scale + 1e-6
    inverse = scale / largest
    coarse = largest.astype(jnp.bfloat16).astype(f32)
    lanes = lax.broadcasted_iota(jnp.int32, (rows, LANES), 1)
    parts = jnp.where(lanes == 0, coarse, jnp.where(lanes == 1, largest - coarse, 0.0))
    parts = parts.astype(jnp.bfloat16)
    for group in range(groups):
        out_ref[group, :, :width] = (rotated_ref[group] * inverse).astype(out_ref.dtype)
        out_ref[group, :, width:] = parts


def transform(hidden, base, sign):
    groups, rows, width = hidden.shape
    low = base.shape[1]
    return pl.pallas_call(
        transform_kernel,
        out_shape=jax.ShapeDtypeStruct((groups, rows, width + LANES), jnp.bfloat16),
        in_specs=[pl.BlockSpec(memory_space=pltpu.VMEM)] * 3,
        out_specs=pl.BlockSpec(memory_space=pltpu.VMEM),
        scratch_shapes=[
            pltpu.VMEM((2, low, TILE), jnp.bfloat16),
            pltpu.VMEM((2, width // low, groups, rows, TILE), jnp.float32),
            pltpu.VMEM((groups, rows, width), jnp.float32),
        ],
        compiler_params=pltpu.CompilerParams(vmem_limit_bytes=VMEM_LIMIT),
        cost_estimate=pl.CostEstimate(
            flops=2 * groups * rows * width * low,
            bytes_accessed=4 * groups * rows * width,
            transcendentals=0,
        ),
        name="rotate_rows",
    )(hidden, base, sign)


def body(gate_pre, up_pre, rotation52):
    steps, rows, width = gate_pre.shape
    groups = lax.axis_size("tensor")
    base, sign = factor(rotation52)
    flat = (steps * rows, width)
    hidden = gated(gate_pre.reshape(flat), up_pre.reshape(flat))
    mine = lax.all_to_all(hidden.reshape(groups, -1, width), "tensor", 0, 0)
    packed = lax.all_to_all(transform(mine, base, sign), "tensor", 0, 0)
    return unpack(packed, steps, rows, width)


def solution(mesh):
    in_specs = (P(None, "dp", "tensor"), P(None, "dp", "tensor"), P())
    out_specs = (P(None, "dp", "tensor"), P(None, "dp"))
    return jax.shard_map(body, mesh=mesh, in_specs=in_specs, out_specs=out_specs, check_vma=False)
```

```python
import jax
import jax.numpy as jnp
from jax import lax
from jax.experimental import pallas as pl
from jax.experimental.pallas import tpu as pltpu
from jax.sharding import PartitionSpec as P

HAD_BIG = 1024
LANES = 128
LOW = 8
PARTS = 4
WINDOW = 512
VMEM_LIMIT = 20 * 1024 * 1024
STREAM_LIMIT = 58 * 1024 * 1024


def hidden_kernel(gate_hbm, up_hbm, out_hbm, gate_ref, up_ref, out_ref, sems):
    chunks, rows, width = gate_ref.shape
    f32 = jnp.float32
    block = 32
    copies = []
    for chunk in range(chunks):
        at = pl.ds(chunk * rows, rows)
        for k, (source, target) in enumerate(((gate_hbm, gate_ref), (up_hbm, up_ref))):
            copy = pltpu.make_async_copy(source.at[at], target.at[chunk], sems.at[chunk, k])
            copy.start()
            copies.append(copy)
    results = []
    for chunk in range(chunks):
        copies[2 * chunk].wait()
        copies[2 * chunk + 1].wait()

        @pl.loop(0, rows // block)
        def _(step):
            at = pl.ds(pl.multiple_of(step * block, block), block)
            gate = gate_ref[chunk, at].astype(f32)
            half = 0.5 * gate
            silu = half * jnp.tanh(half) + half
            out_ref[chunk, at] = (silu * up_ref[chunk, at].astype(f32)).astype(out_ref.dtype)

        at = pl.ds(chunk * rows, rows)
        result = pltpu.make_async_copy(out_ref.at[chunk], out_hbm.at[at], sems.at[chunk, 2])
        result.start()
        results.append(result)
    for result in results:
        result.wait()


def gated(gate, up):
    rows, width = gate.shape
    chunks = 4
    held = pltpu.VMEM((chunks, rows // chunks, width), gate.dtype)
    return pl.pallas_call(
        hidden_kernel,
        out_shape=jax.ShapeDtypeStruct(gate.shape, gate.dtype),
        in_specs=[pl.BlockSpec(memory_space=pl.ANY)] * 2,
        out_specs=pl.BlockSpec(memory_space=pl.ANY),
        scratch_shapes=[held, held, held, pltpu.SemaphoreType.DMA((chunks, 3))],
        compiler_params=pltpu.CompilerParams(vmem_limit_bytes=STREAM_LIMIT),
        cost_estimate=pl.CostEstimate(
            flops=6 * rows * width, bytes_accessed=6 * rows * width, transcendentals=rows * width
        ),
        name="gated_hidden",
    )(gate, up)


def unpack_kernel(packed_ref, out_hbm, peak_ref, sem):
    groups, rows, packed = packed_ref.shape
    width = out_hbm.shape[2]
    steps, span = peak_ref.shape
    per = groups // steps
    copies = []
    count = sem.shape[0]
    for part in range(count):
        at = pl.ds(part * (groups // count), groups // count)
        copy = pltpu.make_async_copy(
            packed_ref.at[at, :, pl.ds(0, width)], out_hbm.at[at], sem.at[part]
        )
        copy.start()
        copies.append(copy)
    lanes = lax.broadcasted_iota(jnp.int32, (8, packed - width), 1)
    both = (lanes < 2).astype(jnp.float32).astype(jnp.bfloat16)
    for step in range(steps):
        parts = packed_ref[step * per : step * per + per, :, width:].reshape(span, packed - width)
        sums = lax.dot_general(
            both, parts, (((1,), (1,)), ((), ())), preferred_element_type=jnp.float32
        )
        peak_ref[step : step + 1, :] = sums[:1]
    for copy in copies:
        copy.wait()


def unpack(packed, steps, span, width):
    quantized, peaks = pl.pallas_call(
        unpack_kernel,
        out_shape=(
            jax.ShapeDtypeStruct((*packed.shape[:2], width), packed.dtype),
            jax.ShapeDtypeStruct((steps, span), jnp.float32),
        ),
        in_specs=[pl.BlockSpec(memory_space=pltpu.VMEM)],
        out_specs=(pl.BlockSpec(memory_space=pl.ANY), pl.BlockSpec(memory_space=pltpu.VMEM)),
        scratch_shapes=[pltpu.SemaphoreType.DMA((4,))],
        compiler_params=pltpu.CompilerParams(vmem_limit_bytes=VMEM_LIMIT),
        name="unpack",
    )(packed)
    return quantized.reshape(steps, span, width), peaks


def parity_sign(left, right):
    both = left & right
    parity = both
    for level in (1, 2):
        parity = parity ^ (both >> level)
    return 1 - 2 * (parity & 1)


def factor_kernel(rotation_ref, out_ref):
    small = rotation_ref.shape[0]
    size = LOW * small
    height, width = out_ref.shape
    margin = height - width
    f32, bf16 = jnp.float32, jnp.bfloat16

    def block(index):
        return (index * 1261) >> 16

    def iota(shape, dim):
        return lax.broadcasted_iota(jnp.int32, shape, dim)

    def one_where(mask):
        return mask.astype(f32).astype(bf16)

    shape = (small, width)
    lane = iota(shape, 1)
    across = one_where((lane - block(lane) * small == iota(shape, 0)) & (lane < size))
    tiled = jnp.dot(rotation_ref[...], across, preferred_element_type=f32).astype(bf16)
    shape = (height, small)
    row = iota(shape, 0) - margin
    inside = (row >= 0) & (row < size)
    down = one_where((row - block(row) * small == iota(shape, 1)) & inside)
    value = jnp.dot(down, tiled, preferred_element_type=f32)
    shape = (height, width)
    sign = parity_sign(block(iota(shape, 0) - margin), block(iota(shape, 1))).astype(f32)
    out_ref[...] = (value * sign).astype(bf16)


def factor(rotation52):
    small = rotation52.shape[0]
    margin = WINDOW - LOW * small
    return pl.pallas_call(
        factor_kernel,
        out_shape=jax.ShapeDtypeStruct((margin + WINDOW, WINDOW), jnp.bfloat16),
        in_specs=[pl.BlockSpec(memory_space=pltpu.VMEM)],
        out_specs=pl.BlockSpec(memory_space=pltpu.VMEM),
        compiler_params=pltpu.CompilerParams(vmem_limit_bytes=VMEM_LIMIT),
        cost_estimate=pl.CostEstimate(
            flops=2 * (margin + WINDOW) * WINDOW * small,
            bytes_accessed=2 * (margin + WINDOW) * WINDOW,
            transcendentals=0,
        ),
        name="kron_factor",
    )(rotation52)


def butterfly(values):
    count = len(values)
    distance = 1
    while distance < count:
        values = [
            values[i] + values[i ^ distance] if i & distance == 0 else values[i ^ distance] - values[i]
            for i in range(count)
        ]
        distance *= 2
    return values


def transform_kernel(hidden_ref, factor_ref, out_ref, product_ref, middle_ref, rotated_ref):
    groups, rows, width = hidden_ref.shape
    margin = factor_ref.shape[0] - WINDOW
    size = WINDOW - margin
    span = PARTS * size
    halves = width // span
    f32 = jnp.float32
    tiles = WINDOW // LANES
    row_tiles = [slice(at, at + 8) for at in range(0, rows, 8)]
    peak = [jnp.zeros((8, LANES), f32) for _ in row_tiles]
    lane = lax.broadcasted_iota(jnp.int32, (8, LANES), 1)

    def multiply(part):
        window = part * size // LANES * LANES
        start = margin - (part * size - window)
        for half in range(halves):
            at = half * span + window
            product_ref[part % 2, half] = jnp.dot(
                hidden_ref[:, :, at : at + WINDOW].reshape(groups * rows, WINDOW),
                factor_ref[start : start + WINDOW, :],
                preferred_element_type=f32,
            ).reshape(groups, rows, WINDOW)

    def combine(part):
        for at in row_tiles:
            for tile in range(tiles):
                column = slice(tile * LANES, (tile + 1) * LANES)
                values = butterfly(
                    [
                        product_ref[part % 2, half, group, at, column]
                        for group in range(groups)
                        for half in range(halves)
                    ]
                )
                for i, value in enumerate(values):
                    group, half = divmod(i, halves)
                    middle_ref[part, half, group, at, column] = value

    def place(group, half, k):
        at = row_tiles[k]
        parts = [[] for _ in range(PARTS)]
        for tile in range(tiles):
            column = slice(tile * LANES, (tile + 1) * LANES)
            values = butterfly([middle_ref[part, half, group, at, column] for part in range(PARTS)])
            for part, value in enumerate(values):
                shift = part * size % LANES
                parts[part].append(pltpu.roll(value, shift, 1) if shift else value)
        placed = []
        for part in range(PARTS):
            shift = part * size % LANES
            values = parts[part]
            if part > 0:
                placed[-1] = jnp.where(lane < shift, placed[-1], values[0])
                values = values[:1] + [
                    jnp.where(lane < shift, values[tile - 1], values[tile]) for tile in range(1, tiles)
                ]
                placed += values[1:]
            else:
                placed += values
        for i, value in enumerate(placed):
            column = half * span + i * LANES
            rotated_ref[group, at, column : column + LANES] = value
        sizes = [jnp.abs(value) for value in placed] + [peak[k]]
        while len(sizes) > 1:
            pairs = [jnp.maximum(*sizes[i : i + 2]) for i in range(0, len(sizes) - 1, 2)]
            sizes = pairs + sizes[2 * len(pairs) :]
        peak[k] = sizes[0]

    multiply(0)
    for part in range(PARTS):
        if part + 1 < PARTS:
            multiply(part + 1)
        combine(part)
    for group in range(groups):
        for half in range(halves):
            for k in range(len(row_tiles)):
                place(group, half, k)
    scale = HAD_BIG**-0.5
    largest = jnp.concatenate([jnp.max(p, axis=1, keepdims=True) for p in peak], axis=0)
    largest = largest * scale + 1e-6
    inverse = scale / largest
    coarse = largest.astype(jnp.bfloat16).astype(f32)
    lanes = lax.broadcasted_iota(jnp.int32, (rows, LANES), 1)
    parts = jnp.where(lanes == 0, coarse, jnp.where(lanes == 1, largest - coarse, 0.0))
    parts = parts.astype(jnp.bfloat16)
    for group in range(groups):
        out_ref[group, :, :width] = (rotated_ref[group] * inverse).astype(out_ref.dtype)
        out_ref[group, :, width:] = parts


def transform(hidden, weights):
    groups, rows, width = hidden.shape
    halves = width // (PARTS * (2 * WINDOW - weights.shape[0]))
    return pl.pallas_call(
        transform_kernel,
        out_shape=jax.ShapeDtypeStruct((groups, rows, width + LANES), jnp.bfloat16),
        in_specs=[pl.BlockSpec(memory_space=pltpu.VMEM)] * 2,
        out_specs=pl.BlockSpec(memory_space=pltpu.VMEM),
        scratch_shapes=[
            pltpu.VMEM((2, halves, groups, rows, WINDOW), jnp.float32),
            pltpu.VMEM((PARTS, halves, groups, rows, WINDOW), jnp.float32),
            pltpu.VMEM((groups, rows, width), jnp.float32),
        ],
        compiler_params=pltpu.CompilerParams(vmem_limit_bytes=VMEM_LIMIT),
        cost_estimate=pl.CostEstimate(
            flops=2 * groups * rows * PARTS * halves * WINDOW * WINDOW,
            bytes_accessed=4 * groups * rows * width,
            transcendentals=0,
        ),
        name="rotate_rows",
    )(hidden, weights)


def body(gate_pre, up_pre, rotation52):
    steps, rows, width = gate_pre.shape
    groups = lax.axis_size("tensor")
    weights = factor(rotation52)
    flat = (steps * rows, width)
    hidden = gated(gate_pre.reshape(flat), up_pre.reshape(flat))
    mine = lax.all_to_all(hidden.reshape(groups, -1, width), "tensor", 0, 0)
    packed = lax.all_to_all(transform(mine, weights), "tensor", 0, 0)
    return unpack(packed, steps, rows, width)


def solution(mesh):
    in_specs = (P(None, "dp", "tensor"), P(None, "dp", "tensor"), P())
    out_specs = (P(None, "dp", "tensor"), P(None, "dp"))
    return jax.shard_map(body, mesh=mesh, in_specs=in_specs, out_specs=out_specs, check_vma=False)
```

```python
import jax
import jax.numpy as jnp
from jax import lax
from jax.experimental import pallas as pl
from jax.experimental.pallas import tpu as pltpu
from jax.sharding import PartitionSpec as P

HAD_BIG = 1024
LANES = 128
LOW = 8
PARTS = 4
WINDOW = 512
SIDE = WINDOW // 2
VMEM_LIMIT = 20 * 1024 * 1024
STREAM_LIMIT = 58 * 1024 * 1024


def hidden_kernel(gate_hbm, up_hbm, out_hbm, gate_ref, up_ref, out_ref, sems):
    chunks, rows, width = gate_ref.shape
    f32 = jnp.float32
    block = 32
    copies = []
    for chunk in range(chunks):
        at = pl.ds(chunk * rows, rows)
        for k, (source, target) in enumerate(((gate_hbm, gate_ref), (up_hbm, up_ref))):
            copy = pltpu.make_async_copy(source.at[at], target.at[chunk], sems.at[chunk, k])
            copy.start()
            copies.append(copy)
    results = []
    for chunk in range(chunks):
        copies[2 * chunk].wait()
        copies[2 * chunk + 1].wait()

        @pl.loop(0, rows // block)
        def _(step):
            at = pl.ds(pl.multiple_of(step * block, block), block)
            gate = gate_ref[chunk, at].astype(f32)
            half = 0.5 * gate
            silu = half * jnp.tanh(half) + half
            out_ref[chunk, at] = (silu * up_ref[chunk, at].astype(f32)).astype(out_ref.dtype)

        at = pl.ds(chunk * rows, rows)
        result = pltpu.make_async_copy(out_ref.at[chunk], out_hbm.at[at], sems.at[chunk, 2])
        result.start()
        results.append(result)
    for result in results:
        result.wait()


def gated(gate, up):
    rows, width = gate.shape
    chunks = 4
    held = pltpu.VMEM((chunks, rows // chunks, width), gate.dtype)
    return pl.pallas_call(
        hidden_kernel,
        out_shape=jax.ShapeDtypeStruct(gate.shape, gate.dtype),
        in_specs=[pl.BlockSpec(memory_space=pl.ANY)] * 2,
        out_specs=pl.BlockSpec(memory_space=pl.ANY),
        scratch_shapes=[held, held, held, pltpu.SemaphoreType.DMA((chunks, 3))],
        compiler_params=pltpu.CompilerParams(vmem_limit_bytes=STREAM_LIMIT),
        cost_estimate=pl.CostEstimate(
            flops=6 * rows * width, bytes_accessed=6 * rows * width, transcendentals=rows * width
        ),
        name="gated_hidden",
    )(gate, up)


def unpack_kernel(packed_ref, out_hbm, peak_ref, held_ref, sems):
    groups, rows, width = held_ref.shape
    steps, span = peak_ref.shape
    count = sems.shape[0]
    each = groups // count
    f32, bf16 = jnp.float32, jnp.bfloat16
    copies = []
    for part in range(count):
        for group in range(part * each, part * each + each):
            for i in range(width // LANES):
                value = packed_ref[group, i * rows : (i + 1) * rows, :]
                held_ref[group, :, i * LANES : (i + 1) * LANES] = value
        at = pl.ds(part * each, each)
        copy = pltpu.make_async_copy(held_ref.at[at], out_hbm.at[at], sems.at[part])
        copy.start()
        copies.append(copy)

    def iota(shape, dim):
        return lax.broadcasted_iota(jnp.int32, shape, dim)

    parts = packed_ref[:, width // LANES * rows :, :].astype(f32).reshape(groups * 8, LANES)
    pick = (iota((8, LANES), 0) == iota((8, LANES), 1)).astype(f32).astype(bf16)
    turned = lax.dot_general(
        pick, parts.astype(bf16), (((1,), (1,)), ((), ())), preferred_element_type=f32
    ).astype(bf16)
    shape = (groups * 8, groups * rows)
    source, target = iota(shape, 0), iota(shape, 1)
    peaks = jnp.zeros((1, groups * rows), f32)
    for k in range(rows // 8):
        place = (target == (source >> 3) * rows + k * 8 + (source & 7)).astype(f32).astype(bf16)
        moved = jnp.dot(turned, place, preferred_element_type=f32)
        peaks = peaks + (moved[2 * k : 2 * k + 1] + moved[2 * k + 1 : 2 * k + 2])
    for step in range(steps):
        peak_ref[step : step + 1, :] = peaks[:, step * span : (step + 1) * span]
    for copy in copies:
        copy.wait()


def unpack(packed, steps, span, width):
    groups = packed.shape[0]
    rows = steps * span // groups
    shape = (groups, rows, width)
    quantized, peaks = pl.pallas_call(
        unpack_kernel,
        out_shape=(
            jax.ShapeDtypeStruct(shape, packed.dtype),
            jax.ShapeDtypeStruct((steps, span), jnp.float32),
        ),
        in_specs=[pl.BlockSpec(memory_space=pltpu.VMEM)],
        out_specs=(pl.BlockSpec(memory_space=pl.ANY), pl.BlockSpec(memory_space=pltpu.VMEM)),
        scratch_shapes=[pltpu.VMEM(shape, packed.dtype), pltpu.SemaphoreType.DMA((4,))],
        compiler_params=pltpu.CompilerParams(vmem_limit_bytes=VMEM_LIMIT),
        name="unpack",
    )(packed)
    return quantized.reshape(steps, span, width), peaks


def parity_sign(left, right):
    both = left & right
    parity = both
    for level in (1, 2):
        parity = parity ^ (both >> level)
    return 1 - 2 * (parity & 1)


def factor_kernel(rotation_ref, out_ref):
    small = rotation_ref.shape[0]
    size = LOW * small
    height, width = out_ref.shape
    margin = height - width
    f32, bf16 = jnp.float32, jnp.bfloat16

    def block(index):
        return (index * 1261) >> 16

    def iota(shape, dim):
        return lax.broadcasted_iota(jnp.int32, shape, dim)

    def one_where(mask):
        return mask.astype(f32).astype(bf16)

    shape = (small, width)
    lane = iota(shape, 1)
    across = one_where((lane - block(lane) * small == iota(shape, 0)) & (lane < size))
    tiled = jnp.dot(rotation_ref[...], across, preferred_element_type=f32).astype(bf16)
    shape = (height, small)
    row = iota(shape, 0) - margin
    inside = (row >= 0) & (row < size)
    down = one_where((row - block(row) * small == iota(shape, 1)) & inside)
    value = jnp.dot(down, tiled, preferred_element_type=f32)
    shape = (height, width)
    sign = parity_sign(block(iota(shape, 0) - margin), block(iota(shape, 1))).astype(f32)
    out_ref[...] = (value * sign).astype(bf16)


def factor(rotation52):
    small = rotation52.shape[0]
    margin = WINDOW - LOW * small
    return pl.pallas_call(
        factor_kernel,
        out_shape=jax.ShapeDtypeStruct((margin + WINDOW, WINDOW), jnp.bfloat16),
        in_specs=[pl.BlockSpec(memory_space=pltpu.VMEM)],
        out_specs=pl.BlockSpec(memory_space=pltpu.VMEM),
        compiler_params=pltpu.CompilerParams(vmem_limit_bytes=VMEM_LIMIT),
        cost_estimate=pl.CostEstimate(
            flops=2 * (margin + WINDOW) * WINDOW * small,
            bytes_accessed=2 * (margin + WINDOW) * WINDOW,
            transcendentals=0,
        ),
        name="kron_factor",
    )(rotation52)


def butterfly(values):
    count = len(values)
    distance = 1
    while distance < count:
        values = [
            values[i] + values[i ^ distance] if i & distance == 0 else values[i ^ distance] - values[i]
            for i in range(count)
        ]
        distance *= 2
    return values


def transform_kernel(hidden_ref, factor_ref, out_ref, product_ref, middle_ref, rotated_ref):
    groups, rows, width = hidden_ref.shape
    margin = factor_ref.shape[0] - WINDOW
    size = WINDOW - margin
    span = PARTS * size
    halves = width // span
    f32 = jnp.float32
    row_tiles = [slice(at, at + 8) for at in range(0, rows, 8)]
    peak = [jnp.zeros((8, LANES), f32) for _ in row_tiles]
    lane = lax.broadcasted_iota(jnp.int32, (8, LANES), 1)

    def multiply(part, side):
        window = part * size // LANES * LANES
        start = margin - (part * size - window)
        for half in range(halves):
            at = half * span + window
            product_ref[part % 2, half] = jnp.dot(
                hidden_ref[:, :, at : at + WINDOW].reshape(groups * rows, WINDOW),
                factor_ref[start : start + WINDOW, side * SIDE : (side + 1) * SIDE],
                preferred_element_type=f32,
            ).reshape(groups, rows, SIDE)

    def combine(part, side):
        for at in row_tiles:
            for tile in range(SIDE // LANES):
                column = slice(tile * LANES, (tile + 1) * LANES)
                values = butterfly(
                    [
                        product_ref[part % 2, half, group, at, column]
                        for group in range(groups)
                        for half in range(halves)
                    ]
                )
                column = slice(side * SIDE + tile * LANES, side * SIDE + (tile + 1) * LANES)
                for i, value in enumerate(values):
                    group, half = divmod(i, halves)
                    middle_ref[part, half, group, at, column] = value

    def place(group, half, k, side):
        at = row_tiles[k]
        shifts = [part * size % LANES for part in range(PARTS)]
        moved = [[] for _ in range(PARTS)]
        for tile in range(2 * side, 2 * side + 2):
            column = slice(tile * LANES, (tile + 1) * LANES)
            values = butterfly([middle_ref[part, half, group, at, column] for part in range(PARTS)])
            for part, value in enumerate(values):
                moved[part].append(pltpu.roll(value, shifts[part], 1) if part else value)

        def tile_at(i):
            column = half * span + i * LANES
            return group, at, slice(column, column + LANES)

        whole = {}
        for part, (left, right) in enumerate(moved):
            first = part * size // LANES
            if side == 0:
                if part == 0:
                    whole[first] = left
                    whole[first + 1] = right
                else:
                    rotated_ref[tile_at(first)] = left
                    whole[first + 1] = jnp.where(lane < shifts[part], left, right)
                    rotated_ref[tile_at(first + 2)] = right
            else:
                if part > 0:
                    waiting = rotated_ref[tile_at(first + 2)]
                    right = jnp.where(lane < shifts[part], left, right)
                    left = jnp.where(lane < shifts[part], waiting, left)
                if part + 1 < PARTS:
                    right = jnp.where(lane < shifts[part + 1], right, rotated_ref[tile_at(first + 3)])
                whole[first + 2] = left
                whole[first + 3] = right
        for i, value in whole.items():
            rotated_ref[tile_at(i)] = value
        sizes = [jnp.abs(value) for value in whole.values()]
        while len(sizes) > 1:
            pairs = [jnp.maximum(*sizes[i : i + 2]) for i in range(0, len(sizes) - 1, 2)]
            sizes = pairs + sizes[2 * len(pairs) :]
        peak[k] = jnp.maximum(peak[k], sizes[0])

    units = [
        (group, half, k)
        for k in range(len(row_tiles))
        for half in range(halves)
        for group in range(groups)
    ]
    steps = [(part, side) for side in range(2) for part in range(PARTS)]
    multiply(*steps[0])
    for i, (part, side) in enumerate(steps):
        if i + 1 < len(steps):
            multiply(*steps[i + 1])
        combine(part, side)
        if side > 0:
            for unit in units[part::PARTS]:
                place(*unit, 0)
    for unit in units:
        place(*unit, 1)
    scale = HAD_BIG**-0.5
    largest = jnp.concatenate([jnp.max(p, axis=1, keepdims=True) for p in peak], axis=0)
    largest = largest * scale + 1e-6
    inverse = scale / largest
    coarse = largest.astype(jnp.bfloat16).astype(f32)
    parts = jnp.zeros((8, LANES), f32)
    for k, at in enumerate(row_tiles):
        parts = jnp.where(lane == 2 * k, coarse[at], parts)
        parts = jnp.where(lane == 2 * k + 1, (largest - coarse)[at], parts)
    parts = parts.astype(jnp.bfloat16)
    for group in range(groups):
        for i in range(width // LANES):
            value = rotated_ref[group, :, i * LANES : (i + 1) * LANES] * inverse
            out_ref[group, i * rows : (i + 1) * rows, :] = value.astype(out_ref.dtype)
        out_ref[group, width // LANES * rows :, :] = parts


def transform(hidden, weights):
    groups, rows, width = hidden.shape
    halves = width // (PARTS * (2 * WINDOW - weights.shape[0]))
    return pl.pallas_call(
        transform_kernel,
        out_shape=jax.ShapeDtypeStruct((groups, width // LANES * rows + 8, LANES), jnp.bfloat16),
        in_specs=[pl.BlockSpec(memory_space=pltpu.VMEM)] * 2,
        out_specs=pl.BlockSpec(memory_space=pltpu.VMEM),
        scratch_shapes=[
            pltpu.VMEM((2, halves, groups, rows, SIDE), jnp.float32),
            pltpu.VMEM((PARTS, halves, groups, rows, WINDOW), jnp.float32),
            pltpu.VMEM((groups, rows, width), jnp.float32),
        ],
        compiler_params=pltpu.CompilerParams(vmem_limit_bytes=VMEM_LIMIT),
        cost_estimate=pl.CostEstimate(
            flops=2 * groups * rows * PARTS * halves * WINDOW * WINDOW,
            bytes_accessed=4 * groups * rows * width,
            transcendentals=0,
        ),
        name="rotate_rows",
    )(hidden, weights)


def body(gate_pre, up_pre, rotation52):
    steps, rows, width = gate_pre.shape
    groups = lax.axis_size("tensor")
    weights = factor(rotation52)
    flat = (steps * rows, width)
    hidden = gated(gate_pre.reshape(flat), up_pre.reshape(flat))
    mine = lax.all_to_all(hidden.reshape(groups, -1, width), "tensor", 0, 0)
    packed = lax.all_to_all(transform(mine, weights), "tensor", 0, 0)
    return unpack(packed, steps, rows, width)


def solution(mesh):
    in_specs = (P(None, "dp", "tensor"), P(None, "dp", "tensor"), P())
    out_specs = (P(None, "dp", "tensor"), P(None, "dp"))
    return jax.shard_map(body, mesh=mesh, in_specs=in_specs, out_specs=out_specs, check_vma=False)
```

```python
import jax
import jax.numpy as jnp
from jax import lax
from jax.experimental import pallas as pl
from jax.experimental.pallas import tpu as pltpu
from jax.sharding import PartitionSpec as P

HAD_BIG = 1024
LANES = 128
LOW = 8
PARTS = 4
WINDOW = 512
SIDE = WINDOW // 2
VMEM_LIMIT = 20 * 1024 * 1024
STREAM_LIMIT = 58 * 1024 * 1024


def hidden_kernel(gate_hbm, up_hbm, out_hbm, gate_ref, up_ref, out_ref, sems):
    chunks, rows, width = gate_ref.shape
    f32 = jnp.float32
    block = 32
    copies = []
    for chunk in range(chunks):
        at = pl.ds(chunk * rows, rows)
        for k, (source, target) in enumerate(((gate_hbm, gate_ref), (up_hbm, up_ref))):
            copy = pltpu.make_async_copy(source.at[at], target.at[chunk], sems.at[chunk, k])
            copy.start()
            copies.append(copy)
    results = []
    for chunk in range(chunks):
        copies[2 * chunk].wait()
        copies[2 * chunk + 1].wait()

        @pl.loop(0, rows // block)
        def _(step):
            at = pl.ds(pl.multiple_of(step * block, block), block)
            gate = gate_ref[chunk, at].astype(f32)
            half = 0.5 * gate
            silu = half * jnp.tanh(half) + half
            out_ref[chunk, at] = (silu * up_ref[chunk, at].astype(f32)).astype(out_ref.dtype)

        at = pl.ds(chunk * rows, rows)
        result = pltpu.make_async_copy(out_ref.at[chunk], out_hbm.at[at], sems.at[chunk, 2])
        result.start()
        results.append(result)
    for result in results:
        result.wait()


def gated(gate, up):
    rows, width = gate.shape
    chunks = 4
    held = pltpu.VMEM((chunks, rows // chunks, width), gate.dtype)
    return pl.pallas_call(
        hidden_kernel,
        out_shape=jax.ShapeDtypeStruct(gate.shape, gate.dtype),
        in_specs=[pl.BlockSpec(memory_space=pl.ANY)] * 2,
        out_specs=pl.BlockSpec(memory_space=pl.ANY),
        scratch_shapes=[held, held, held, pltpu.SemaphoreType.DMA((chunks, 3))],
        compiler_params=pltpu.CompilerParams(vmem_limit_bytes=STREAM_LIMIT),
        cost_estimate=pl.CostEstimate(
            flops=6 * rows * width, bytes_accessed=6 * rows * width, transcendentals=rows * width
        ),
        name="gated_hidden",
    )(gate, up)


def packet_rows(i, rows, tiles):
    start = i * rows + (8 if i == tiles - 1 else 0)
    return slice(start, start + rows)


def peak_rows(rows, tiles):
    return slice((tiles - 1) * rows, (tiles - 1) * rows + 8)


def unpack_kernel(packed_ref, out_hbm, peak_ref, held_ref, sems):
    groups, rows, width = held_ref.shape
    steps, span = peak_ref.shape
    count = sems.shape[0]
    each = groups // count
    f32, bf16 = jnp.float32, jnp.bfloat16
    copies = []
    for part in range(count):
        for group in range(part * each, part * each + each):
            for i in range(width // LANES):
                value = packed_ref[group, packet_rows(i, rows, width // LANES), :]
                held_ref[group, :, i * LANES : (i + 1) * LANES] = value
        at = pl.ds(part * each, each)
        copy = pltpu.make_async_copy(held_ref.at[at], out_hbm.at[at], sems.at[part])
        copy.start()
        copies.append(copy)

    def iota(shape, dim):
        return lax.broadcasted_iota(jnp.int32, shape, dim)

    parts = packed_ref[:, peak_rows(rows, width // LANES), :].astype(f32).reshape(groups * 8, LANES)
    pick = (iota((8, LANES), 0) == iota((8, LANES), 1)).astype(f32).astype(bf16)
    turned = lax.dot_general(
        pick, parts.astype(bf16), (((1,), (1,)), ((), ())), preferred_element_type=f32
    ).astype(bf16)
    shape = (groups * 8, groups * rows)
    source, target = iota(shape, 0), iota(shape, 1)
    peaks = jnp.zeros((1, groups * rows), f32)
    for k in range(rows // 8):
        place = (target == (source >> 3) * rows + k * 8 + (source & 7)).astype(f32).astype(bf16)
        moved = jnp.dot(turned, place, preferred_element_type=f32)
        peaks = peaks + (moved[2 * k : 2 * k + 1] + moved[2 * k + 1 : 2 * k + 2])
    for step in range(steps):
        peak_ref[step : step + 1, :] = peaks[:, step * span : (step + 1) * span]
    for copy in copies:
        copy.wait()


def unpack(packed, steps, span, width):
    groups = packed.shape[0]
    rows = steps * span // groups
    shape = (groups, rows, width)
    quantized, peaks = pl.pallas_call(
        unpack_kernel,
        out_shape=(
            jax.ShapeDtypeStruct(shape, packed.dtype),
            jax.ShapeDtypeStruct((steps, span), jnp.float32),
        ),
        in_specs=[pl.BlockSpec(memory_space=pltpu.VMEM)],
        out_specs=(pl.BlockSpec(memory_space=pl.ANY), pl.BlockSpec(memory_space=pltpu.VMEM)),
        scratch_shapes=[pltpu.VMEM(shape, packed.dtype), pltpu.SemaphoreType.DMA((4,))],
        compiler_params=pltpu.CompilerParams(vmem_limit_bytes=VMEM_LIMIT),
        name="unpack",
    )(packed)
    return quantized.reshape(steps, span, width), peaks


def parity_sign(left, right):
    both = left & right
    parity = both
    for level in (1, 2):
        parity = parity ^ (both >> level)
    return 1 - 2 * (parity & 1)


def factor_kernel(rotation_ref, out_ref):
    small = rotation_ref.shape[0]
    size = LOW * small
    height, width = out_ref.shape
    margin = height - width
    f32, bf16 = jnp.float32, jnp.bfloat16

    def block(index):
        return (index * 1261) >> 16

    def iota(shape, dim):
        return lax.broadcasted_iota(jnp.int32, shape, dim)

    def one_where(mask):
        return mask.astype(f32).astype(bf16)

    shape = (small, width)
    lane = iota(shape, 1)
    across = one_where((lane - block(lane) * small == iota(shape, 0)) & (lane < size))
    tiled = jnp.dot(rotation_ref[...], across, preferred_element_type=f32).astype(bf16)
    shape = (height, small)
    row = iota(shape, 0) - margin
    inside = (row >= 0) & (row < size)
    down = one_where((row - block(row) * small == iota(shape, 1)) & inside)
    value = jnp.dot(down, tiled, preferred_element_type=f32)
    shape = (height, width)
    sign = parity_sign(block(iota(shape, 0) - margin), block(iota(shape, 1))).astype(f32)
    out_ref[...] = (value * sign).astype(bf16)


def factor(rotation52):
    small = rotation52.shape[0]
    margin = WINDOW - LOW * small
    return pl.pallas_call(
        factor_kernel,
        out_shape=jax.ShapeDtypeStruct((margin + WINDOW, WINDOW), jnp.bfloat16),
        in_specs=[pl.BlockSpec(memory_space=pltpu.VMEM)],
        out_specs=pl.BlockSpec(memory_space=pltpu.VMEM),
        compiler_params=pltpu.CompilerParams(vmem_limit_bytes=VMEM_LIMIT),
        cost_estimate=pl.CostEstimate(
            flops=2 * (margin + WINDOW) * WINDOW * small,
            bytes_accessed=2 * (margin + WINDOW) * WINDOW,
            transcendentals=0,
        ),
        name="kron_factor",
    )(rotation52)


def butterfly(values):
    count = len(values)
    distance = 1
    while distance < count:
        values = [
            values[i] + values[i ^ distance] if i & distance == 0 else values[i ^ distance] - values[i]
            for i in range(count)
        ]
        distance *= 2
    return values


def transform_kernel(hidden_ref, factor_ref, out_ref, product_ref, middle_ref, rotated_ref):
    groups, rows, width = hidden_ref.shape
    margin = factor_ref.shape[0] - WINDOW
    size = WINDOW - margin
    span = PARTS * size
    halves = width // span
    f32 = jnp.float32
    row_tiles = [slice(at, at + 8) for at in range(0, rows, 8)]
    peak = [jnp.zeros((8, LANES), f32) for _ in row_tiles]
    lane = lax.broadcasted_iota(jnp.int32, (8, LANES), 1)

    def multiply(part, side):
        window = part * size // LANES * LANES
        start = margin - (part * size - window)
        for half in range(halves):
            at = half * span + window
            product_ref[part % 2, half] = jnp.dot(
                hidden_ref[:, :, at : at + WINDOW].reshape(groups * rows, WINDOW),
                factor_ref[start : start + WINDOW, side * SIDE : (side + 1) * SIDE],
                preferred_element_type=f32,
            ).reshape(groups, rows, SIDE)

    def combine(part, side):
        for at in row_tiles:
            for tile in range(SIDE // LANES):
                column = slice(tile * LANES, (tile + 1) * LANES)
                values = butterfly(
                    [
                        product_ref[part % 2, half, group, at, column]
                        for group in range(groups)
                        for half in range(halves)
                    ]
                )
                column = slice(side * SIDE + tile * LANES, side * SIDE + (tile + 1) * LANES)
                for i, value in enumerate(values):
                    group, half = divmod(i, halves)
                    middle_ref[part, half, group, at, column] = value

    def place(group, half, k, side):
        at = row_tiles[k]
        shifts = [part * size % LANES for part in range(PARTS)]
        moved = [[] for _ in range(PARTS)]
        for tile in range(2 * side, 2 * side + 2):
            column = slice(tile * LANES, (tile + 1) * LANES)
            values = butterfly([middle_ref[part, half, group, at, column] for part in range(PARTS)])
            for part, value in enumerate(values):
                moved[part].append(pltpu.roll(value, shifts[part], 1) if part else value)

        def tile_at(i):
            column = half * span + i * LANES
            return group, at, slice(column, column + LANES)

        whole = {}
        for part, (left, right) in enumerate(moved):
            first = part * size // LANES
            if side == 0:
                if part == 0:
                    whole[first] = left
                    whole[first + 1] = right
                else:
                    rotated_ref[tile_at(first)] = left
                    whole[first + 1] = jnp.where(lane < shifts[part], left, right)
                    rotated_ref[tile_at(first + 2)] = right
            else:
                if part > 0:
                    waiting = rotated_ref[tile_at(first + 2)]
                    right = jnp.where(lane < shifts[part], left, right)
                    left = jnp.where(lane < shifts[part], waiting, left)
                if part + 1 < PARTS:
                    right = jnp.where(lane < shifts[part + 1], right, rotated_ref[tile_at(first + 3)])
                whole[first + 2] = left
                whole[first + 3] = right
        for i, value in whole.items():
            rotated_ref[tile_at(i)] = value
        sizes = [jnp.abs(value) for value in whole.values()]
        while len(sizes) > 1:
            pairs = [jnp.maximum(*sizes[i : i + 2]) for i in range(0, len(sizes) - 1, 2)]
            sizes = pairs + sizes[2 * len(pairs) :]
        peak[k] = jnp.maximum(peak[k], sizes[0])

    units = [
        (group, half, k)
        for k in range(len(row_tiles))
        for half in range(halves)
        for group in range(groups)
    ]
    steps = [(part, side) for side in range(2) for part in range(PARTS)]
    multiply(*steps[0])
    for i, (part, side) in enumerate(steps):
        if i + 1 < len(steps):
            multiply(*steps[i + 1])
        combine(part, side)
        if side > 0:
            for unit in units[part::PARTS]:
                place(*unit, 0)
    for unit in units:
        place(*unit, 1)
    scale = HAD_BIG**-0.5
    largest = jnp.concatenate([jnp.max(p, axis=1, keepdims=True) for p in peak], axis=0)
    largest = largest * scale + 1e-6
    inverse = scale / largest
    coarse = largest.astype(jnp.bfloat16).astype(f32)
    parts = jnp.zeros((8, LANES), f32)
    for k, at in enumerate(row_tiles):
        parts = jnp.where(lane == 2 * k, coarse[at], parts)
        parts = jnp.where(lane == 2 * k + 1, (largest - coarse)[at], parts)
    parts = parts.astype(jnp.bfloat16)
    for group in range(groups):
        for i in range(width // LANES):
            value = rotated_ref[group, :, i * LANES : (i + 1) * LANES] * inverse
            out_ref[group, packet_rows(i, rows, width // LANES), :] = value.astype(out_ref.dtype)
        out_ref[group, peak_rows(rows, width // LANES), :] = parts


def transform(hidden, weights):
    groups, rows, width = hidden.shape
    halves = width // (PARTS * (2 * WINDOW - weights.shape[0]))
    return pl.pallas_call(
        transform_kernel,
        out_shape=jax.ShapeDtypeStruct((groups, width // LANES * rows + 8, LANES), jnp.bfloat16),
        in_specs=[pl.BlockSpec(memory_space=pltpu.VMEM)] * 2,
        out_specs=pl.BlockSpec(memory_space=pltpu.VMEM),
        scratch_shapes=[
            pltpu.VMEM((2, halves, groups, rows, SIDE), jnp.float32),
            pltpu.VMEM((PARTS, halves, groups, rows, WINDOW), jnp.float32),
            pltpu.VMEM((groups, rows, width), jnp.float32),
        ],
        compiler_params=pltpu.CompilerParams(vmem_limit_bytes=VMEM_LIMIT),
        cost_estimate=pl.CostEstimate(
            flops=2 * groups * rows * PARTS * halves * WINDOW * WINDOW,
            bytes_accessed=4 * groups * rows * width,
            transcendentals=0,
        ),
        name="rotate_rows",
    )(hidden, weights)


def body(gate_pre, up_pre, rotation52):
    steps, rows, width = gate_pre.shape
    groups = lax.axis_size("tensor")
    weights = factor(rotation52)
    flat = (steps * rows, width)
    hidden = gated(gate_pre.reshape(flat), up_pre.reshape(flat))
    mine = lax.all_to_all(hidden.reshape(groups, -1, width), "tensor", 0, 0)
    packed = lax.all_to_all(transform(mine, weights), "tensor", 0, 0)
    return unpack(packed, steps, rows, width)


def solution(mesh):
    in_specs = (P(None, "dp", "tensor"), P(None, "dp", "tensor"), P())
    out_specs = (P(None, "dp", "tensor"), P(None, "dp"))
    return jax.shard_map(body, mesh=mesh, in_specs=in_specs, out_specs=out_specs, check_vma=False)
```

```python
import jax
import jax.numpy as jnp
from jax import lax
from jax.experimental import pallas as pl
from jax.experimental.pallas import tpu as pltpu
from jax.sharding import PartitionSpec as P

HAD_BIG = 1024
LANES = 128
LOW = 8
PARTS = 4
WINDOW = 512
SIDE = WINDOW // 2
VMEM_LIMIT = 20 * 1024 * 1024
STREAM_LIMIT = 51 * 1024 * 1024


def parity_sign(left, right):
    both = left & right
    parity = both
    for level in (1, 2):
        parity = parity ^ (both >> level)
    return 1 - 2 * (parity & 1)


def write_factor(rotation, out_ref):
    small = rotation.shape[0]
    size = LOW * small
    height, width = out_ref.shape
    margin = height - width
    f32, bf16 = jnp.float32, jnp.bfloat16

    def block(index):
        return (index * 1261) >> 16

    def iota(shape, dim):
        return lax.broadcasted_iota(jnp.int32, shape, dim)

    def one_where(mask):
        return mask.astype(f32).astype(bf16)

    shape = (small, width)
    lane = iota(shape, 1)
    across = one_where((lane - block(lane) * small == iota(shape, 0)) & (lane < size))
    tiled = jnp.dot(rotation, across, preferred_element_type=f32).astype(bf16)
    shape = (height, small)
    row = iota(shape, 0) - margin
    inside = (row >= 0) & (row < size)
    down = one_where((row - block(row) * small == iota(shape, 1)) & inside)
    value = jnp.dot(down, tiled, preferred_element_type=f32)
    shape = (height, width)
    sign = parity_sign(block(iota(shape, 0) - margin), block(iota(shape, 1))).astype(f32)
    out_ref[...] = (value * sign).astype(bf16)


def hidden_kernel(
    gate_hbm, up_hbm, rotation_hbm, out_ref, factor_ref, gate_ref, up_ref, rotation_ref, sems, own_sem
):
    chunks, rows, width = gate_ref.shape
    f32 = jnp.float32
    block = 32
    own = pltpu.make_async_copy(rotation_hbm, rotation_ref, own_sem)
    own.start()
    copies = []
    for chunk in range(chunks):
        at = pl.ds(chunk * rows, rows)
        for k, (source, target) in enumerate(((gate_hbm, gate_ref), (up_hbm, up_ref))):
            copy = pltpu.make_async_copy(source.at[at], target.at[chunk], sems.at[chunk, k])
            copy.start()
            copies.append(copy)
    own.wait()
    write_factor(rotation_ref[...], factor_ref)
    for chunk in range(chunks):
        copies[2 * chunk].wait()
        copies[2 * chunk + 1].wait()

        @pl.loop(0, rows // block)
        def _(step):
            at = pl.ds(pl.multiple_of(step * block, block), block)
            gate = gate_ref[chunk, at].astype(f32)
            half = 0.5 * gate
            silu = half * jnp.tanh(half) + half
            value = (silu * up_ref[chunk, at].astype(f32)).astype(out_ref.dtype)
            each = out_ref.shape[1]
            into = pl.ds(chunk * (rows // each) + step * (block // each), block // each)
            out_ref[into] = value.reshape(block // each, each, width)


def gated(gate, up, rotation52, groups):
    rows, width = gate.shape
    small = rotation52.shape[0]
    margin = WINDOW - LOW * small
    chunks = 4
    held = pltpu.VMEM((chunks, rows // chunks, width), gate.dtype)
    return pl.pallas_call(
        hidden_kernel,
        out_shape=(
            jax.ShapeDtypeStruct((groups, rows // groups, width), gate.dtype),
            jax.ShapeDtypeStruct((margin + WINDOW, WINDOW), jnp.bfloat16),
        ),
        in_specs=[pl.BlockSpec(memory_space=pl.ANY)] * 3,
        out_specs=[pl.BlockSpec(memory_space=pltpu.VMEM)] * 2,
        scratch_shapes=[
            held,
            held,
            pltpu.VMEM((small, small), rotation52.dtype),
            pltpu.SemaphoreType.DMA((chunks, 2)),
            pltpu.SemaphoreType.DMA,
        ],
        compiler_params=pltpu.CompilerParams(vmem_limit_bytes=STREAM_LIMIT),
        cost_estimate=pl.CostEstimate(
            flops=6 * rows * width, bytes_accessed=6 * rows * width, transcendentals=rows * width
        ),
        name="gated_hidden",
    )(gate, up, rotation52)


def packet_rows(i, rows, tiles):
    start = i * rows + (8 if i == tiles - 1 else 0)
    return slice(start, start + rows)


def peak_rows(rows, tiles):
    return slice((tiles - 1) * rows, (tiles - 1) * rows + 8)


def unpack_kernel(packed_ref, out_hbm, peak_ref, held_ref, sems):
    groups, rows, width = held_ref.shape
    steps, span = peak_ref.shape
    count = sems.shape[0]
    each = groups // count
    f32, bf16 = jnp.float32, jnp.bfloat16
    copies = []
    for part in range(count):
        for group in range(part * each, part * each + each):
            for i in range(width // LANES):
                value = packed_ref[group, packet_rows(i, rows, width // LANES), :]
                held_ref[group, :, i * LANES : (i + 1) * LANES] = value
        at = pl.ds(part * each, each)
        copy = pltpu.make_async_copy(held_ref.at[at], out_hbm.at[at], sems.at[part])
        copy.start()
        copies.append(copy)

    def iota(shape, dim):
        return lax.broadcasted_iota(jnp.int32, shape, dim)

    parts = packed_ref[:, peak_rows(rows, width // LANES), :].astype(f32).reshape(groups * 8, LANES)
    pick = (iota((8, LANES), 0) == iota((8, LANES), 1)).astype(f32).astype(bf16)
    turned = lax.dot_general(
        pick, parts.astype(bf16), (((1,), (1,)), ((), ())), preferred_element_type=f32
    ).astype(bf16)
    shape = (groups * 8, groups * rows)
    source, target = iota(shape, 0), iota(shape, 1)
    peaks = jnp.zeros((1, groups * rows), f32)
    for k in range(rows // 8):
        place = (target == (source >> 3) * rows + k * 8 + (source & 7)).astype(f32).astype(bf16)
        moved = jnp.dot(turned, place, preferred_element_type=f32)
        peaks = peaks + (moved[2 * k : 2 * k + 1] + moved[2 * k + 1 : 2 * k + 2])
    for step in range(steps):
        peak_ref[step : step + 1, :] = peaks[:, step * span : (step + 1) * span]
    for copy in copies:
        copy.wait()


def unpack(packed, steps, span, width):
    groups = packed.shape[0]
    rows = steps * span // groups
    shape = (groups, rows, width)
    quantized, peaks = pl.pallas_call(
        unpack_kernel,
        out_shape=(
            jax.ShapeDtypeStruct(shape, packed.dtype),
            jax.ShapeDtypeStruct((steps, span), jnp.float32),
        ),
        in_specs=[pl.BlockSpec(memory_space=pltpu.VMEM)],
        out_specs=(pl.BlockSpec(memory_space=pl.ANY), pl.BlockSpec(memory_space=pltpu.VMEM)),
        scratch_shapes=[pltpu.VMEM(shape, packed.dtype), pltpu.SemaphoreType.DMA((4,))],
        compiler_params=pltpu.CompilerParams(vmem_limit_bytes=VMEM_LIMIT),
        name="unpack",
    )(packed)
    return quantized.reshape(steps, span, width), peaks


def butterfly(values):
    count = len(values)
    distance = 1
    while distance < count:
        values = [
            values[i] + values[i ^ distance] if i & distance == 0 else values[i ^ distance] - values[i]
            for i in range(count)
        ]
        distance *= 2
    return values


def transform_kernel(hidden_ref, factor_ref, out_ref, product_ref, middle_ref, rotated_ref):
    groups, rows, width = hidden_ref.shape
    margin = factor_ref.shape[0] - WINDOW
    size = WINDOW - margin
    span = PARTS * size
    halves = width // span
    f32 = jnp.float32
    row_tiles = [slice(at, at + 8) for at in range(0, rows, 8)]
    peak = [jnp.zeros((8, LANES), f32) for _ in row_tiles]
    lane = lax.broadcasted_iota(jnp.int32, (8, LANES), 1)

    def multiply(part, side):
        window = part * size // LANES * LANES
        start = margin - (part * size - window)
        for half in range(halves):
            at = half * span + window
            product_ref[part % 2, half] = jnp.dot(
                hidden_ref[:, :, at : at + WINDOW].reshape(groups * rows, WINDOW),
                factor_ref[start : start + WINDOW, side * SIDE : (side + 1) * SIDE],
                preferred_element_type=f32,
            ).reshape(groups, rows, SIDE)

    def combine(part, side):
        for at in row_tiles:
            for tile in range(SIDE // LANES):
                column = slice(tile * LANES, (tile + 1) * LANES)
                values = butterfly(
                    [
                        product_ref[part % 2, half, group, at, column]
                        for group in range(groups)
                        for half in range(halves)
                    ]
                )
                column = slice(side * SIDE + tile * LANES, side * SIDE + (tile + 1) * LANES)
                for i, value in enumerate(values):
                    group, half = divmod(i, halves)
                    middle_ref[part, half, group, at, column] = value

    def place(group, half, k, side):
        at = row_tiles[k]
        shifts = [part * size % LANES for part in range(PARTS)]
        moved = [[] for _ in range(PARTS)]
        for tile in range(2 * side, 2 * side + 2):
            column = slice(tile * LANES, (tile + 1) * LANES)
            values = butterfly([middle_ref[part, half, group, at, column] for part in range(PARTS)])
            for part, value in enumerate(values):
                moved[part].append(pltpu.roll(value, shifts[part], 1) if part else value)

        def tile_at(i):
            column = half * span + i * LANES
            return group, at, slice(column, column + LANES)

        whole = {}
        for part, (left, right) in enumerate(moved):
            first = part * size // LANES
            if side == 0:
                if part == 0:
                    whole[first] = left
                    whole[first + 1] = right
                else:
                    rotated_ref[tile_at(first)] = left
                    whole[first + 1] = jnp.where(lane < shifts[part], left, right)
                    rotated_ref[tile_at(first + 2)] = right
            else:
                if part > 0:
                    waiting = rotated_ref[tile_at(first + 2)]
                    right = jnp.where(lane < shifts[part], left, right)
                    left = jnp.where(lane < shifts[part], waiting, left)
                if part + 1 < PARTS:
                    right = jnp.where(lane < shifts[part + 1], right, rotated_ref[tile_at(first + 3)])
                whole[first + 2] = left
                whole[first + 3] = right
        for i, value in whole.items():
            rotated_ref[tile_at(i)] = value
        sizes = [jnp.abs(value) for value in whole.values()]
        while len(sizes) > 1:
            pairs = [jnp.maximum(*sizes[i : i + 2]) for i in range(0, len(sizes) - 1, 2)]
            sizes = pairs + sizes[2 * len(pairs) :]
        peak[k] = jnp.maximum(peak[k], sizes[0])

    units = [
        (group, half, k)
        for k in range(len(row_tiles))
        for half in range(halves)
        for group in range(groups)
    ]
    steps = [(part, side) for side in range(2) for part in range(PARTS)]
    multiply(*steps[0])
    for i, (part, side) in enumerate(steps):
        if i + 1 < len(steps):
            multiply(*steps[i + 1])
        combine(part, side)
        if side > 0:
            for unit in units[part::PARTS]:
                place(*unit, 0)
    for unit in units:
        place(*unit, 1)
    scale = HAD_BIG**-0.5
    largest = jnp.concatenate([jnp.max(p, axis=1, keepdims=True) for p in peak], axis=0)
    largest = largest * scale + 1e-6
    inverse = scale / largest
    coarse = largest.astype(jnp.bfloat16).astype(f32)
    parts = jnp.zeros((8, LANES), f32)
    for k, at in enumerate(row_tiles):
        parts = jnp.where(lane == 2 * k, coarse[at], parts)
        parts = jnp.where(lane == 2 * k + 1, (largest - coarse)[at], parts)
    parts = parts.astype(jnp.bfloat16)
    for group in range(groups):
        for i in range(width // LANES):
            value = rotated_ref[group, :, i * LANES : (i + 1) * LANES] * inverse
            out_ref[group, packet_rows(i, rows, width // LANES), :] = value.astype(out_ref.dtype)
        out_ref[group, peak_rows(rows, width // LANES), :] = parts


def transform(hidden, weights):
    groups, rows, width = hidden.shape
    halves = width // (PARTS * (2 * WINDOW - weights.shape[0]))
    return pl.pallas_call(
        transform_kernel,
        out_shape=jax.ShapeDtypeStruct((groups, width // LANES * rows + 8, LANES), jnp.bfloat16),
        in_specs=[pl.BlockSpec(memory_space=pltpu.VMEM)] * 2,
        out_specs=pl.BlockSpec(memory_space=pltpu.VMEM),
        scratch_shapes=[
            pltpu.VMEM((2, halves, groups, rows, SIDE), jnp.float32),
            pltpu.VMEM((PARTS, halves, groups, rows, WINDOW), jnp.float32),
            pltpu.VMEM((groups, rows, width), jnp.float32),
        ],
        compiler_params=pltpu.CompilerParams(vmem_limit_bytes=VMEM_LIMIT),
        cost_estimate=pl.CostEstimate(
            flops=2 * groups * rows * PARTS * halves * WINDOW * WINDOW,
            bytes_accessed=4 * groups * rows * width,
            transcendentals=0,
        ),
        name="rotate_rows",
    )(hidden, weights)


def body(gate_pre, up_pre, rotation52):
    steps, rows, width = gate_pre.shape
    groups = lax.axis_size("tensor")
    flat = (steps * rows, width)
    hidden, weights = gated(gate_pre.reshape(flat), up_pre.reshape(flat), rotation52, groups)
    mine = lax.all_to_all(hidden, "tensor", 0, 0)
    packed = lax.all_to_all(transform(mine, weights), "tensor", 0, 0)
    return unpack(packed, steps, rows, width)


def solution(mesh):
    in_specs = (P(None, "dp", "tensor"), P(None, "dp", "tensor"), P())
    out_specs = (P(None, "dp", "tensor"), P(None, "dp"))
    return jax.shard_map(body, mesh=mesh, in_specs=in_specs, out_specs=out_specs, check_vma=False)
```
